32 devices in a mesh: dp: 1, seq: 32 (over z, y, x, core).
Axes of the slice: x: 2, y: 2, z: 4, core: 2. Of those that a mesh axis runs over, the one named last changes fastest.
Arguments:
- queries: bfloat16 [1, 4096, 1024], P('dp', 'seq'), may hold values from -6 to 6
- keys: bfloat16 [1, 4096, 1024], P('dp', 'seq'), may hold values from -6 to 6
- values: bfloat16 [1, 4096, 1024], P('dp', 'seq'), may hold values from -6 to 6
- gates: bfloat16 [1, 4096, 1024], P('dp', 'seq'), may hold values from -6 to 6
- cotangent: bfloat16 [1, 4096, 1024], P('dp', 'seq'), may hold values from -6 to 6
- segment: int32 [1, 4096], P('dp'), may hold values from 0 to 15, never falling along the last dimension, each value on 1 to 1024 neighbouring positions
- w_out: bfloat16 [1024, 1024], replicated, may hold values from -0.1875 to 0.1875
Outputs:
- output: bfloat16 [1, 4096, 1024], P('dp', 'seq')
- grad_queries: bfloat16 [1, 4096, 1024], P('dp', 'seq')
- grad_keys: bfloat16 [1, 4096, 1024], P('dp', 'seq')
- grad_values: bfloat16 [1, 4096, 1024], P('dp', 'seq')
- grad_gates: bfloat16 [1, 4096, 1024], P('dp', 'seq')
- grad_w_out: float32 [1024, 1024], P(('dp', 'seq'))
The draws below stay inside these ranges and needn't reach their ends.
Inputs may be any that keep to these rules, and one draw needn't show every extreme that they name: `segment`: within each replica the user numbers never fall along the tokens; every user has 1 to 1024 tokens, and one user has exactly 1024.
All inputs are finite; a program needn't handle non-finite values.
Results may differ from the reference program's by a relative error of at most 0.0058.
Values may be sent and summed in bfloat16 or wider, within the bound.
A program may use at most 128 MiB of HBM per device.

```python
import math
import jax
import jax.numpy as jnp
import numpy as np
from jax import lax

HEADS = 8
WIDTH = 1024
TOK_DEV = 128
LMAX = 1024
HOPS = 8
COUNT = 16
SEQ_TOKENS = 4096
N_DP = 1


def spiked(values, rng, source, target, shards_of, factor):
    owner, partner = [(jnp.arange(values.shape[position]) // (values.shape[position] // shards_of)).reshape([-1 if axis == position else 1 for axis in range(values.ndim)]) for position in (source, target)]
    chosen = jax.random.permutation(rng, shards_of)[partner]
    strong = (owner == chosen) | (owner == (partner + shards_of // 2) % shards_of)
    return jnp.where(strong, factor * values, values)


def levels(stream_key, extent, pieces, least, top_value):
    def one(dim, parts):
        draws = jax.random.uniform(jax.random.fold_in(jax.random.fold_in(stream_key, 6), dim), (parts,), jnp.float32, least / len(pieces), top_value / len(pieces))
        return jnp.repeat(jnp.exp(draws), extent[dim] // parts).reshape((-1,) + (1,) * (len(extent) - dim - 1))

    level = one(*pieces[0])
    for cut in pieces[1:]:
        level = level * one(*cut)
    return level


def length_profile(number_of, total, most, slope):
    portions = [(1 << 20) // math.isqrt(rank ** slope) + 1 for rank in range(2, number_of + 1)]
    rest, holding = total - most - (number_of - 1), [1] * (number_of - 1)
    while rest > 0:
        movable = [i for i in range(number_of - 1) if holding[i] < most]
        mass, remaining = sum([portions[i] for i in movable]), rest
        for i in movable:
            extra = min(most - holding[i], max(1, remaining * portions[i] // mass), rest)
            holding[i] = holding[i] + extra
            rest = rest - extra
    return np.array([most] + holding)


def uneven_parts(rng, number_of, total, most, skew):
    if number_of == 2:
        one = jax.random.randint(rng, (), max(1, total - most), min(most, total - 1) + 1)
        return jnp.stack([one, total - one])
    tallies = jnp.asarray(length_profile(number_of, total, most, skew), jnp.int32)
    couples = (number_of - 1) // 2
    donor, receiver = tallies[1:1 + 2 * couples:2], tallies[2:2 + 2 * couples:2]
    room = jnp.minimum(donor - 1, most - receiver)
    moved = jax.random.randint(jax.random.fold_in(rng, 1), (couples,), 0, 1 << 20) % (room + 1)
    tallies = tallies.at[1:1 + 2 * couples:2].set(donor - moved).at[2:2 + 2 * couples:2].set(receiver + moved)
    return tallies[jax.random.permutation(jax.random.fold_in(rng, 2), number_of)]


def bell_draw(rng, dims, deviation, bound, pieces=(), held_as=jnp.bfloat16):
    array = jax.random.normal(rng, dims, jnp.float32) * deviation
    if len(pieces) > 0:
        array = levels(rng, dims, pieces, -0.22, 0.18) * array
    return jnp.clip(array, min=-bound, max=bound).astype(held_as)


def heavy_noise(rng, extent, scale, reach, pieces, heavy, held_as=jnp.bfloat16):
    values = scale * jax.random.normal(rng, extent, jnp.float32)
    if pieces:
        values = values * levels(rng, extent, pieces, -0.22, 0.18)
    return jnp.clip(spiked(values, jax.random.fold_in(rng, 3), *heavy), -reach, reach).astype(held_as)


def setup_inputs(seed: int = 0) -> dict:
    key_list = jax.random.split(jax.random.key(seed), 8)
    queries = bell_draw(key_list[0], (N_DP, SEQ_TOKENS, WIDTH), 1.0, 6.0, ((1, 32),))
    keys = bell_draw(key_list[1], (N_DP, SEQ_TOKENS, WIDTH), 1.0, 6.0, ((1, 32),))
    values = bell_draw(key_list[2], (N_DP, SEQ_TOKENS, WIDTH), 1.0, 6.0, ((1, 32),))
    gates = bell_draw(key_list[3], (N_DP, SEQ_TOKENS, WIDTH), 1.0, 6.0, ((1, 32),))
    cotangent = heavy_noise(key_list[4], (N_DP, SEQ_TOKENS, WIDTH), 1.0, 6.0, ((1, 32),), (1, 2, 32, 2.75))
    segment = jax.vmap(lambda own: jnp.searchsorted(jnp.cumsum(uneven_parts(own, COUNT, SEQ_TOKENS, LMAX, 2)), jnp.arange(SEQ_TOKENS), side="right"))(jax.random.split(key_list[5], N_DP)).reshape((N_DP, SEQ_TOKENS)).astype(jnp.int32)
    w_out = bell_draw(key_list[6], (WIDTH, WIDTH), WIDTH ** -0.5, 0.1875)
    return dict(queries=queries, keys=keys, values=values, gates=gates, cotangent=cotangent, segment=segment, w_out=w_out)


EPS = 1e-05

def silu_slope(scores):
    sigmoid_value = jax.nn.sigmoid(scores)
    return sigmoid_value * (1.0 + scores * (1.0 - sigmoid_value))

def block_pass(query_rows, gate_rows, cotan_rows, w_out, key_rows, value_rows, allowed):
    row_count, features = query_rows.shape
    head_size = features // HEADS
    score_scale = 1.0 / math.sqrt(head_size)
    query_heads = query_rows.astype(jnp.float32).reshape(row_count, HEADS, head_size)
    key_heads = key_rows.astype(jnp.float32).reshape(-1, HEADS, head_size)
    value_heads = value_rows.astype(jnp.float32).reshape(-1, HEADS, head_size)
    scores = jnp.einsum('qhd,khd->hqk', query_heads, key_heads) * score_scale
    weights = jnp.where(allowed[None], jax.nn.silu(scores), 0.0).astype(jnp.bfloat16)
    mixed = jnp.einsum('hqk,khd->qhd', weights.astype(jnp.float32), value_heads).reshape(row_count, features)
    row_mean = lax.optimization_barrier(jnp.mean(mixed, axis=-1, keepdims=True))
    centred = mixed - row_mean
    inverse = lax.rsqrt(lax.optimization_barrier(jnp.mean(centred * centred, axis=-1, keepdims=True)) + EPS)
    normed = centred * inverse
    gate_float = gate_rows.astype(jnp.float32)
    gated = (normed * gate_float).astype(jnp.bfloat16)
    output_rows = jnp.dot(gated, w_out, preferred_element_type=jnp.float32).astype(jnp.bfloat16)
    dgated = jnp.dot(cotan_rows, w_out.T, preferred_element_type=jnp.float32)
    grad_gate_rows = (dgated * normed).astype(jnp.bfloat16)
    dnormed = dgated * gate_float
    dmixed = inverse * (dnormed - lax.optimization_barrier(jnp.mean(dnormed, axis=-1, keepdims=True)) - normed * lax.optimization_barrier(jnp.mean(dnormed * normed, axis=-1, keepdims=True)))
    dmixed = dmixed.astype(jnp.bfloat16)
    dmixed_heads = dmixed.astype(jnp.float32).reshape(row_count, HEADS, head_size)
    dweights = jnp.einsum('qhd,khd->hqk', dmixed_heads, value_heads)
    dscores = jnp.where(allowed[None], dweights * silu_slope(scores) * score_scale, 0.0).astype(jnp.bfloat16)
    dvalue_rows = jnp.einsum('hqk,qhd->khd', weights.astype(jnp.float32), dmixed_heads).reshape(-1, features)
    dquery_rows = jnp.einsum('hqk,khd->qhd', dscores.astype(jnp.float32), key_heads).reshape(row_count, features)
    dkey_rows = jnp.einsum('hqk,qhd->khd', dscores.astype(jnp.float32), query_heads).reshape(-1, features)
    weight_part = jnp.dot(gated.T, cotan_rows, preferred_element_type=jnp.float32)
    return (output_rows, dquery_rows.astype(jnp.bfloat16), grad_gate_rows, dkey_rows, dvalue_rows, weight_part)

def reference(queries, keys, values, gates, cotangent, segment, w_out):
    groups, total_rows, features = queries.shape
    reach_rows = HOPS * TOK_DEV
    key_count = reach_rows + TOK_DEV
    block_total = total_rows // TOK_DEV

    def one_group(arrays):
        query_all, key_all, value_all, gate_all, cotan_all, segment_ids = arrays
        keys_padded = jnp.concatenate([jnp.zeros((reach_rows, features), jnp.bfloat16), key_all])
        values_padded = jnp.concatenate([jnp.zeros((reach_rows, features), jnp.bfloat16), value_all])
        segment_padded = jnp.concatenate([jnp.full((reach_rows,), -1, jnp.int32), segment_ids])

        def block_step(running, block_index):
            dkey_acc, dvalue_acc, weight_acc = running
            block_start = (block_index * TOK_DEV).astype(jnp.int32)
            query_rows = lax.dynamic_slice_in_dim(query_all, block_start, TOK_DEV)
            gate_rows = lax.dynamic_slice_in_dim(gate_all, block_start, TOK_DEV)
            cotan_rows = lax.dynamic_slice_in_dim(cotan_all, block_start, TOK_DEV)
            key_rows = lax.dynamic_slice_in_dim(keys_padded, block_start, key_count)
            value_rows = lax.dynamic_slice_in_dim(values_padded, block_start, key_count)
            key_segment = lax.dynamic_slice_in_dim(segment_padded, block_start, key_count)
            query_segment = lax.dynamic_slice_in_dim(segment_ids, block_start, TOK_DEV)
            query_place = block_start + jnp.arange(TOK_DEV, dtype=jnp.int32)
            key_place = block_start - reach_rows + jnp.arange(key_count, dtype=jnp.int32)
            allowed = (query_segment[:, None] == key_segment[None, :]) & (key_place[None, :] <= query_place[:, None])
            output_rows, dquery_rows, grad_gate_rows, dkey_rows, dvalue_rows, weight_part = block_pass(query_rows, gate_rows, cotan_rows, w_out, key_rows, value_rows, allowed)
            dkey_acc = lax.dynamic_update_slice_in_dim(dkey_acc, lax.dynamic_slice_in_dim(dkey_acc, block_start, key_count) + dkey_rows, block_start, 0)
            dvalue_acc = lax.dynamic_update_slice_in_dim(dvalue_acc, lax.dynamic_slice_in_dim(dvalue_acc, block_start, key_count) + dvalue_rows, block_start, 0)
            return ((dkey_acc, dvalue_acc, weight_acc + weight_part), (output_rows, dquery_rows, grad_gate_rows))
        start_state = (jnp.zeros((total_rows + reach_rows, features), jnp.float32), jnp.zeros((total_rows + reach_rows, features), jnp.float32), jnp.zeros((features, features), jnp.float32))
        final_state, stacked = lax.scan(block_step, start_state, jnp.arange(block_total, dtype=jnp.int32))
        dkey_acc, dvalue_acc, weight_acc = final_state
        output_all = stacked[0].reshape(total_rows, features)
        dquery_all = stacked[1].reshape(total_rows, features)
        dgate_all = stacked[2].reshape(total_rows, features)
        return (output_all, dquery_all, dkey_acc[reach_rows:].astype(jnp.bfloat16), dvalue_acc[reach_rows:].astype(jnp.bfloat16), dgate_all, weight_acc)
    results = lax.map(one_group, (queries, keys, values, gates, cotangent, segment))
    return (results[0], results[1], results[2], results[3], results[4], lax.optimization_barrier(jnp.sum(results[5], axis=0)))
```

```python
import functools
import math

import jax
import jax.numpy as jnp
from jax import lax
from jax.experimental import pallas as pl
from jax.experimental.pallas import tpu as pltpu
from jax.sharding import PartitionSpec as P

HEADS = 8
EPS = 1e-05
F32 = jnp.float32
BF16 = jnp.bfloat16


def dot_nn(a, b):
    return lax.dot_general(a, b, (((1,), (0,)), ((), ())), preferred_element_type=F32)


def dot_nt(a, b):
    return lax.dot_general(a, b, (((1,), (1,)), ((), ())), preferred_element_type=F32)


def dot_tn(a, b):
    return lax.dot_general(a, b, (((0,), (0,)), ((), ())), preferred_element_type=F32)


def kernel(
    groups,
    q_ref, k_ref, v_ref, gate_ref, cot_ref, w_ref, segrow_ref, segcol_ref,
    out_ref, dq_ref, dk_ref, dv_ref, dgate_ref, wpart_ref,
    qh, kh, vh, wts, slope, mix_stage, mix_in, dgated, gated, dmix_stage, dmh,
    dq_stage, dk_acc, dv_acc, dk_stage, dv_stage, dq_in, own_in, next_in,
    s_qkv, r_qkv, s_nxt, r_nxt, s_mix, r_mix, s_dm, r_dm, s_dq, r_dq, s_own, r_own, s_prv, r_prv,
):
    rows = q_ref.shape[0]
    features = q_ref.shape[1]
    hd = features // HEADS
    span = HEADS * rows
    win = span + rows
    scale = 1.0 / math.sqrt(hd)
    me = lax.axis_index("seq")
    g = me // HEADS
    p = lax.rem(me, HEADS)
    base = g * HEADS
    has_prev = g > 0
    has_next = g < groups - 1

    def rs(i):
        return pl.ds(pl.multiple_of(i * rows, rows), rows)

    def cs(i):
        return pl.ds(pl.multiple_of(i * hd, hd), hd)

    def peer(o):
        return lax.rem(p + o, HEADS)

    def source(o):
        return lax.rem(p + HEADS - o, HEADS)

    def copy(src, dst, ss, rsem, dev):
        return pltpu.make_async_remote_copy(
            src_ref=src, dst_ref=dst, send_sem=ss, recv_sem=rsem,
            device_id={"seq": dev}, device_id_type=pl.DeviceIdType.MESH,
        )

    barrier = pltpu.get_barrier_semaphore()

    def greet(dev):
        pl.semaphore_signal(
            barrier, inc=1, device_id={"seq": dev}, device_id_type=pl.DeviceIdType.MESH
        )

    for o in range(1, HEADS):
        greet(base + peer(o))

    @pl.when(has_next)
    def _():
        for o in range(HEADS):
            greet(base + HEADS + peer(o))

    @pl.when(has_prev)
    def _():
        for o in range(HEADS):
            greet(base - HEADS + peer(o))

    sides = jnp.minimum(g, 1) + jnp.minimum(groups - 1 - g, 1)
    pl.semaphore_wait(barrier, HEADS - 1 + HEADS * sides)

    ins = ((k_ref, kh, HEADS), (v_ref, vh, HEADS), (q_ref, qh, 0))

    def qkv_copy(kind, o, where):
        src, dst, off = ins[kind]
        return copy(src.at[:, cs(peer(o))], dst.at[rs(off + where)],
                    s_qkv.at[kind, o], r_qkv.at[kind, o], base + peer(o))

    def nxt_copy(kind, o, where):
        src, dst, _ = ins[kind]
        return copy(src.at[:, cs(peer(o))], dst.at[rs(where)],
                    s_nxt.at[kind, o], r_nxt.at[kind, o], base + HEADS + peer(o))

    @pl.when(has_next)
    def _():
        for kind in range(2):
            for o in range(HEADS):
                nxt_copy(kind, o, p).start()

    for kind in range(3):
        for o in range(1, HEADS):
            qkv_copy(kind, o, p).start()
    for src, dst, off in ins:
        dst[rs(off + p), :] = src[:, cs(p)]

    @pl.when(jnp.logical_not(has_prev))
    def _():
        kh[pl.ds(0, span), :] = jnp.zeros((span, hd), BF16)
        vh[pl.ds(0, span), :] = jnp.zeros((span, hd), BF16)

    dgated[...] = dot_nt(cot_ref[...], w_ref[...])
    dk_acc[...] = jnp.zeros_like(dk_acc)
    dv_acc[...] = jnp.zeros_like(dv_acc)

    for kind in range(3):
        for o in range(1, HEADS):
            qkv_copy(kind, o, source(o)).wait_recv()

    @pl.when(has_prev)
    def _():
        for kind in range(2):
            for o in range(HEADS):
                nxt_copy(kind, o, source(o)).wait_recv()

    def mix_copy(o, b, col):
        return copy(mix_stage.at[rs(b)], mix_in.at[:, cs(col)],
                    s_mix.at[o], r_mix.at[o], base + peer(o))

    def forward(i, carry):
        o = i + 1
        b = peer(o)
        win_rows = pl.ds(pl.multiple_of(b * rows, rows), win)
        scores = dot_nt(qh[rs(b), :], kh[win_rows, :]) * scale
        qi = lax.broadcasted_iota(jnp.int32, (rows, win), 0)
        kj = lax.broadcasted_iota(jnp.int32, (rows, win), 1)
        allowed = (segcol_ref[rs(b), :] == segrow_ref[:, win_rows]) & (kj - span <= qi)
        sig = 1.0 / (1.0 + jnp.exp(-scores))
        w = jnp.where(allowed, scores * sig, 0.0).astype(BF16)
        wts[rs(b), :] = w
        slope[rs(b), :] = jnp.where(
            allowed, (scale * sig) * (1.0 + scores * (1.0 - sig)), 0.0
        )
        mix_stage[rs(b), :] = dot_nn(w, vh[win_rows, :])

        @pl.when(o < HEADS)
        def _():
            mix_copy(o, b, p).start()

        return carry

    lax.fori_loop(0, HEADS, forward, 0)
    mix_in[:, cs(p)] = mix_stage[rs(p), :]
    for o in range(1, HEADS):
        mix_copy(o, p, source(o)).wait_recv()

    mixed = mix_in[...]
    centred = mixed - jnp.mean(mixed, axis=-1, keepdims=True)
    inverse = lax.rsqrt(jnp.mean(centred * centred, axis=-1, keepdims=True) + EPS)
    normed = centred * inverse
    gate = gate_ref[...].astype(F32)
    dg = dgated[...]
    dnormed = dg * gate
    dmixed = inverse * (
        dnormed
        - jnp.mean(dnormed, axis=-1, keepdims=True)
        - normed * jnp.mean(dnormed * normed, axis=-1, keepdims=True)
    )
    dmix_stage[...] = dmixed.astype(BF16)

    def dm_copy(o, where):
        return copy(dmix_stage.at[:, cs(peer(o))], dmh.at[rs(where)],
                    s_dm.at[o], r_dm.at[o], base + peer(o))

    for o in range(1, HEADS):
        dm_copy(o, p).start()
    dmh[rs(p), :] = dmix_stage[:, cs(p)]
    dgate_ref[...] = (dg * normed).astype(BF16)
    gated[...] = (normed * gate).astype(BF16)
    out_ref[...] = dot_nn(gated[...], w_ref[...]).astype(BF16)

    def weight_chunk(c, carry):
        wpart_ref[rs(c), :] = dot_tn(gated[:, cs(c)], cot_ref[...])
        return carry

    lax.fori_loop(0, HEADS, weight_chunk, 0)
    for o in range(1, HEADS):
        dm_copy(o, source(o)).wait_recv()

    grads = ((dk_acc, dk_stage), (dv_acc, dv_stage))

    def dq_copy(b, dev, col):
        return copy(dq_stage.at[rs(b)], dq_in.at[:, cs(col)], s_dq.at[b], r_dq.at[col], base + dev)

    def prv_copy(kind, b, col):
        return copy(grads[kind][1].at[rs(b)], next_in.at[kind, :, cs(col)],
                    s_prv.at[kind, b], r_prv.at[kind, col], base - HEADS + b)

    def own_copy(kind, b, dev, col):
        return copy(grads[kind][1].at[rs(HEADS + b)], own_in.at[kind, :, cs(col)],
                    s_own.at[kind, b], r_own.at[kind, col], base + dev)

    def backward(b, carry):
        win_rows = pl.ds(pl.multiple_of(b * rows, rows), win)
        dm = dmh[rs(b), :]
        ds = (dot_nt(dm, vh[win_rows, :]) * slope[rs(b), :]).astype(BF16)
        dq_stage[rs(b), :] = dot_nn(ds, kh[win_rows, :]).astype(BF16)

        @pl.when(b != p)
        def _():
            dq_copy(b, b, p).start()

        dk_acc[win_rows, :] += dot_tn(ds, qh[rs(b), :])
        dv_acc[win_rows, :] += dot_tn(wts[rs(b), :], dm)
        for acc, stage in grads:
            stage[rs(b), :] = acc[rs(b), :].astype(BF16)

        @pl.when(has_prev)
        def _():
            for kind in range(2):
                prv_copy(kind, b, p).start()

        return carry

    lax.fori_loop(0, HEADS, backward, 0)
    for acc, stage in grads:
        stage[pl.ds(span, span), :] = acc[pl.ds(span, span), :].astype(BF16)
    for kind in range(2):
        for o in range(1, HEADS):
            own_copy(kind, peer(o), peer(o), p).start()
        own_in[kind, :, cs(p)] = grads[kind][1][rs(HEADS + p), :]
    dq_in[:, cs(p)] = dq_stage[rs(p), :]

    @pl.when(jnp.logical_not(has_next))
    def _():
        next_in[...] = jnp.zeros_like(next_in)

    for o in range(1, HEADS):
        dq_copy(peer(o), peer(o), source(o)).wait_recv()
    dq_ref[...] = dq_in[...]

    @pl.when(has_next)
    def _():
        for kind in range(2):
            for o in range(HEADS):
                prv_copy(kind, peer(o), source(o)).wait_recv()

    for kind in range(2):
        for o in range(1, HEADS):
            own_copy(kind, peer(o), peer(o), source(o)).wait_recv()
    for kind, ref in ((0, dk_ref), (1, dv_ref)):
        ref[...] = (own_in[kind].astype(F32) + next_in[kind].astype(F32)).astype(BF16)

    @pl.when(has_next)
    def _():
        for kind in range(2):
            for o in range(HEADS):
                nxt_copy(kind, o, p).wait_send()

    @pl.when(has_prev)
    def _():
        for kind in range(2):
            for o in range(HEADS):
                prv_copy(kind, peer(o), p).wait_send()

    for o in range(1, HEADS):
        for kind in range(3):
            qkv_copy(kind, o, p).wait_send()
        mix_copy(o, peer(o), p).wait_send()
        dm_copy(o, p).wait_send()
        dq_copy(peer(o), peer(o), p).wait_send()
        for kind in range(2):
            own_copy(kind, peer(o), peer(o), p).wait_send()


def shards(queries, keys, values, gates, cotangent, segment, w_out):
    rows, features = queries.shape[1:]
    hd = features // HEADS
    span = HEADS * rows
    groups = lax.axis_size("seq") // HEADS
    g = lax.axis_index("seq") // HEADS
    padded = jnp.concatenate([jnp.full((span,), -1, jnp.int32), segment[0]])
    seg_win = lax.dynamic_slice_in_dim(padded, g * span, 2 * span)
    vm = pl.BlockSpec(memory_space=pltpu.VMEM)
    token = jax.ShapeDtypeStruct((rows, features), BF16)
    dma = pltpu.SemaphoreType.DMA
    results = pl.pallas_call(
        functools.partial(kernel, groups),
        out_shape=(token,) * 5 + (jax.ShapeDtypeStruct((features, features), F32),),
        in_specs=[vm] * 8,
        out_specs=(vm,) * 6,
        scratch_shapes=[
            pltpu.VMEM((span, hd), BF16),
            pltpu.VMEM((2 * span, hd), BF16),
            pltpu.VMEM((2 * span, hd), BF16),
            pltpu.VMEM((span, span + rows), BF16),
            pltpu.VMEM((span, span + rows), F32),
            pltpu.VMEM((span, hd), F32),
            pltpu.VMEM((rows, features), F32),
            pltpu.VMEM((rows, features), F32),
            pltpu.VMEM((rows, features), BF16),
            pltpu.VMEM((rows, features), BF16),
            pltpu.VMEM((span, hd), BF16),
            pltpu.VMEM((span, hd), BF16),
            pltpu.VMEM((2 * span, hd), F32),
            pltpu.VMEM((2 * span, hd), F32),
            pltpu.VMEM((2 * span, hd), BF16),
            pltpu.VMEM((2 * span, hd), BF16),
            pltpu.VMEM((rows, features), BF16),
            pltpu.VMEM((2, rows, features), BF16),
            pltpu.VMEM((2, rows, features), BF16),
            dma((3, HEADS)), dma((3, HEADS)),
            dma((2, HEADS)), dma((2, HEADS)),
            dma((HEADS,)), dma((HEADS,)),
            dma((HEADS,)), dma((HEADS,)),
            dma((HEADS,)), dma((HEADS,)),
            dma((2, HEADS)), dma((2, HEADS)),
            dma((2, HEADS)), dma((2, HEADS)),
        ],
        compiler_params=pltpu.CompilerParams(
            collective_id=0, has_side_effects=True, vmem_limit_bytes=48 * 1024 * 1024
        ),
        cost_estimate=pl.CostEstimate(
            flops=3_000_000_000, bytes_accessed=12_000_000, transcendentals=1_200_000
        ),
    )(
        queries[0], keys[0], values[0], gates[0], cotangent[0], w_out,
        seg_win[None], seg_win[span:, None],
    )
    output, dq, dk, dv, dgate, weight_part = results
    weight_grad = lax.psum_scatter(weight_part, ("dp", "seq"), scatter_dimension=0, tiled=True)
    return output[None], dq[None], dk[None], dv[None], dgate[None], weight_grad


def solution(mesh):
    tokens = P("dp", "seq", None)
    return jax.shard_map(
        shards,
        mesh=mesh,
        in_specs=(tokens,) * 5 + (P("dp", None), P()),
        out_specs=(tokens,) * 5 + (P(("dp", "seq"), None),),
        check_vma=False,
    )
```

```python
import functools
import math

import jax
import jax.numpy as jnp
from jax import lax
from jax.experimental import pallas as pl
from jax.experimental.pallas import tpu as pltpu
from jax.sharding import PartitionSpec as P

HEADS = 8
EPS = 1e-05
F32 = jnp.float32
BF16 = jnp.bfloat16


def dot_nn(a, b):
    return lax.dot_general(a, b, (((1,), (0,)), ((), ())), preferred_element_type=F32)


def dot_nt(a, b):
    return lax.dot_general(a, b, (((1,), (1,)), ((), ())), preferred_element_type=F32)


def dot_tn(a, b):
    return lax.dot_general(a, b, (((0,), (0,)), ((), ())), preferred_element_type=F32)


def kernel(
    groups, fused,
    q_ref, k_ref, v_ref, gate_hbm, cot_hbm, w_hbm, seg_ref,
    out_ref, dq_ref, dk_ref, dv_ref, dgate_ref, wgrad_ref,
    gate_ref, cot_ref, w_ref, result, wresult, seg_win,
    qh, kh, vh, wts, slope, mix_stage, mix_in, dgated, gated, dmix_stage, dmh,
    dq_stage, dk_acc, dv_acc, dk_stage, dv_stage, dq_in, own_in, next_in,
    part, part_send, pair_in, chip_acc, chip_send, chip_in, level_acc, level_send, level_in,
    s_qkv, r_qkv, s_nxt, r_nxt, s_mix, r_mix, s_dm, r_dm, s_dq, r_dq, s_own, r_own, s_prv, r_prv,
    s_pair, r_pair, s_chip, r_chip, s_level, r_level, s_load, s_store,
):
    rows = q_ref.shape[0]
    features = q_ref.shape[1]
    hd = features // HEADS
    span = HEADS * rows
    win = span + rows
    scale = 1.0 / math.sqrt(hd)
    me = lax.axis_index("seq")
    g = me // HEADS
    p = lax.rem(me, HEADS)
    base = g * HEADS
    has_prev = g > 0
    has_next = g < groups - 1
    core = lax.rem(p, 2)
    chip = p // 2
    chips = HEADS // 2

    def rs(i):
        return pl.ds(pl.multiple_of(i * rows, rows), rows)

    def cs(i):
        return pl.ds(pl.multiple_of(i * hd, hd), hd)

    def peer(o):
        return lax.rem(p + o, HEADS)

    def source(o):
        return lax.rem(p + HEADS - o, HEADS)

    def copy(src, dst, ss, rsem, dev):
        return pltpu.make_async_remote_copy(
            src_ref=src, dst_ref=dst, send_sem=ss, recv_sem=rsem,
            device_id={"seq": dev}, device_id_type=pl.DeviceIdType.MESH,
        )

    barrier = pltpu.get_barrier_semaphore()

    def greet(dev):
        pl.semaphore_signal(
            barrier, inc=1, device_id={"seq": dev}, device_id_type=pl.DeviceIdType.MESH
        )

    for o in range(1, HEADS):
        greet(base + peer(o))

    @pl.when(has_next)
    def _():
        for o in range(HEADS):
            greet(base + HEADS + peer(o))

    @pl.when(has_prev)
    def _():
        for o in range(HEADS):
            greet(base - HEADS + peer(o))

    def level(o):
        return lax.rem(g + o, groups)

    def level_source(o):
        return lax.rem(g + groups - o, groups)

    sides = jnp.minimum(g, 1) + jnp.minimum(groups - 1 - g, 1)
    greeted = HEADS - 1 + HEADS * sides
    if fused:
        for o in range(1, groups):

            @pl.when(jnp.abs(level(o) - g) > 1)
            def _():
                greet(level(o) * HEADS + p)

        greeted = greeted + groups - 1 - sides
    loads = [
        pltpu.make_async_copy(src, dst, s_load.at[i])
        for i, (src, dst) in enumerate(
            (
                (cot_hbm, cot_ref), (w_hbm, w_ref), (gate_hbm, gate_ref),
                (k_ref.at[:, cs(p)], kh.at[rs(HEADS + p)]),
                (v_ref.at[:, cs(p)], vh.at[rs(HEADS + p)]),
                (q_ref.at[:, cs(p)], qh.at[rs(p)]),
            )
        )
    ]
    for load in loads:
        load.start()
    pl.semaphore_wait(barrier, greeted)

    ins = ((k_ref, kh, HEADS), (v_ref, vh, HEADS), (q_ref, qh, 0))

    def qkv_copy(kind, o, where):
        src, dst, off = ins[kind]
        return copy(src.at[:, cs(peer(o))], dst.at[rs(off + where)],
                    s_qkv.at[kind, o], r_qkv.at[kind, o], base + peer(o))

    def nxt_copy(kind, o, where):
        src, dst, _ = ins[kind]
        return copy(src.at[:, cs(peer(o))], dst.at[rs(where)],
                    s_nxt.at[kind, o], r_nxt.at[kind, o], base + HEADS + peer(o))

    @pl.when(has_next)
    def _():
        for kind in range(2):
            for o in range(HEADS):
                nxt_copy(kind, o, p).start()

    for kind in range(3):
        for o in range(1, HEADS):
            qkv_copy(kind, o, p).start()
    seg_own = seg_ref[:, pl.ds(pl.multiple_of(g * span, span), span)]
    seg_before = seg_ref[:, pl.ds(pl.multiple_of(jnp.maximum(g - 1, 0) * span, span), span)]
    seg_win[:, pl.ds(span, span)] = seg_own
    seg_win[:, pl.ds(0, span)] = jnp.where(has_prev, seg_before, -1)

    @pl.when(jnp.logical_not(has_prev))
    def _():
        kh[pl.ds(0, span), :] = jnp.zeros((span, hd), BF16)
        vh[pl.ds(0, span), :] = jnp.zeros((span, hd), BF16)

    for load in loads:
        load.wait()
    dgated[...] = dot_nt(cot_ref[...], w_ref[...])
    dk_acc[...] = jnp.zeros_like(dk_acc)
    dv_acc[...] = jnp.zeros_like(dv_acc)

    for kind in range(3):
        for o in range(1, HEADS):
            qkv_copy(kind, o, source(o)).wait_recv()

    @pl.when(has_prev)
    def _():
        for kind in range(2):
            for o in range(HEADS):
                nxt_copy(kind, o, source(o)).wait_recv()

    def mix_copy(o, b, col):
        return copy(mix_stage.at[rs(b)], mix_in.at[:, cs(col)],
                    s_mix.at[o], r_mix.at[o], base + peer(o))

    def forward(i, carry):
        o = i + 1
        b = peer(o)
        win_rows = pl.ds(pl.multiple_of(b * rows, rows), win)
        scores = dot_nt(qh[rs(b), :], kh[win_rows, :]) * scale
        qi = lax.broadcasted_iota(jnp.int32, (rows, win), 0)
        kj = lax.broadcasted_iota(jnp.int32, (rows, win), 1)
        seg_q = seg_win[:, pl.ds(pl.multiple_of(span + b * rows, rows), rows)]
        seg_q = jnp.transpose(jnp.broadcast_to(seg_q, (rows, rows)))[:, :1]
        allowed = (seg_q == seg_win[:, win_rows]) & (kj - span <= qi)
        sig = 1.0 / (1.0 + jnp.exp(-scores))
        w = jnp.where(allowed, scores * sig, 0.0).astype(BF16)
        wts[rs(b), :] = w
        slope[rs(b), :] = jnp.where(
            allowed, (scale * sig) * (1.0 + scores * (1.0 - sig)), 0.0
        )
        mix_stage[rs(b), :] = dot_nn(w, vh[win_rows, :])

        @pl.when(o < HEADS)
        def _():
            mix_copy(o, b, p).start()

        return carry

    lax.fori_loop(0, HEADS, forward, 0)
    mix_in[:, cs(p)] = mix_stage[rs(p), :]
    for o in range(1, HEADS):
        mix_copy(o, p, source(o)).wait_recv()

    mixed = mix_in[...]
    centred = mixed - jnp.mean(mixed, axis=-1, keepdims=True)
    inverse = lax.rsqrt(jnp.mean(centred * centred, axis=-1, keepdims=True) + EPS)
    normed = centred * inverse
    gate = gate_ref[...].astype(F32)
    dg = dgated[...]
    dnormed = dg * gate
    dmixed = inverse * (
        dnormed
        - jnp.mean(dnormed, axis=-1, keepdims=True)
        - normed * jnp.mean(dnormed * normed, axis=-1, keepdims=True)
    )
    dmix_stage[...] = dmixed.astype(BF16)

    def dm_copy(o, where):
        return copy(dmix_stage.at[:, cs(peer(o))], dmh.at[rs(where)],
                    s_dm.at[o], r_dm.at[o], base + peer(o))

    for o in range(1, HEADS):
        dm_copy(o, p).start()
    dmh[rs(p), :] = dmix_stage[:, cs(p)]
    gated[...] = (normed * gate).astype(BF16)
    def chip_copy(o, where):
        there = lax.rem(chip + o, chips)
        return copy(chip_send.at[there], chip_in.at[where],
                    s_chip.at[o], r_chip.at[o], base + 2 * there + core)

    def level_copy(o, where):
        return copy(level_send.at[level(o)], level_in.at[where],
                    s_level.at[o], r_level.at[o], level(o) * HEADS + p)

    if fused:
        pair_copy = copy(part_send.at[1 - core], pair_in, s_pair, r_pair, base + p + 1 - 2 * core)
        share = part.shape[3]
        block = HEADS * share
        for i in range(groups):
            product = dot_tn(gated[:, i * block : (i + 1) * block], cot_ref[...])
            for j in range(HEADS):
                piece = product[j * share : (j + 1) * share]
                part[j % 2, j // 2, i] = piece
                part_send[j % 2, j // 2, i] = piece.astype(BF16)
        pair_copy.start()
    else:

        def weight_chunk(c, carry):
            wresult[rs(c), :] = dot_tn(gated[:, cs(c)], cot_ref[...])
            return carry

        lax.fori_loop(0, HEADS, weight_chunk, 0)
    result[4] = (dg * normed).astype(BF16)
    result[0] = dot_nn(gated[...], w_ref[...]).astype(BF16)
    outs = (out_ref, dq_ref, dk_ref, dv_ref, dgate_ref)
    stores = [
        pltpu.make_async_copy(result.at[i], ref, s_store.at[i]) for i, ref in enumerate(outs)
    ]
    stores.append(pltpu.make_async_copy(wresult, wgrad_ref, s_store.at[5]))
    stores[0].start()
    stores[4].start()
    if fused:
        pair_copy.wait_recv()
        for o in range(1, chips):
            there = lax.rem(chip + o, chips)
            chip_send[there] = (part[core, there] + pair_in[there].astype(F32)).astype(BF16)
            chip_copy(o, chip).start()
        chip_acc[...] = part[core, chip] + pair_in[chip].astype(F32)
    for o in range(1, HEADS):
        dm_copy(o, source(o)).wait_recv()

    grads = ((dk_acc, dk_stage), (dv_acc, dv_stage))

    def dq_copy(b, dev, col):
        return copy(dq_stage.at[rs(b)], dq_in.at[:, cs(col)], s_dq.at[b], r_dq.at[col], base + dev)

    def prv_copy(kind, b, col):
        return copy(grads[kind][1].at[rs(b)], next_in.at[kind, :, cs(col)],
                    s_prv.at[kind, b], r_prv.at[kind, col], base - HEADS + b)

    def own_copy(kind, b, dev, col):
        return copy(grads[kind][1].at[rs(HEADS + b)], own_in.at[kind, :, cs(col)],
                    s_own.at[kind, b], r_own.at[kind, col], base + dev)

    def backward(b, carry):
        win_rows = pl.ds(pl.multiple_of(b * rows, rows), win)
        dm = dmh[rs(b), :]
        ds = (dot_nt(dm, vh[win_rows, :]) * slope[rs(b), :]).astype(BF16)
        dq_stage[rs(b), :] = dot_nn(ds, kh[win_rows, :]).astype(BF16)

        @pl.when(b != p)
        def _():
            dq_copy(b, b, p).start()

        dk_acc[win_rows, :] += dot_tn(ds, qh[rs(b), :])
        dv_acc[win_rows, :] += dot_tn(wts[rs(b), :], dm)
        for acc, stage in grads:
            stage[rs(b), :] = acc[rs(b), :].astype(BF16)

        @pl.when(has_prev)
        def _():
            for kind in range(2):
                prv_copy(kind, b, p).start()

        return carry

    lax.fori_loop(0, HEADS, backward, 0)
    for acc, stage in grads:
        stage[pl.ds(span, span), :] = acc[pl.ds(span, span), :].astype(BF16)
    for kind in range(2):
        for o in range(1, HEADS):
            own_copy(kind, peer(o), peer(o), p).start()
        own_in[kind, :, cs(p)] = grads[kind][1][rs(HEADS + p), :]
    dq_in[:, cs(p)] = dq_stage[rs(p), :]

    if fused:
        total = chip_acc[...]
        for o in range(1, chips):
            there = lax.rem(chip + chips - o, chips)
            chip_copy(o, there).wait_recv()
            total = total + chip_in[there].astype(F32)
        level_acc[...] = total
        level_send[...] = total.astype(BF16)
        for o in range(1, groups):
            level_copy(o, g).start()

    @pl.when(jnp.logical_not(has_next))
    def _():
        next_in[...] = jnp.zeros_like(next_in)

    for o in range(1, HEADS):
        dq_copy(peer(o), peer(o), source(o)).wait_recv()
    result[1] = dq_in[...]
    stores[1].start()

    @pl.when(has_next)
    def _():
        for kind in range(2):
            for o in range(HEADS):
                prv_copy(kind, peer(o), source(o)).wait_recv()

    for kind in range(2):
        for o in range(1, HEADS):
            own_copy(kind, peer(o), peer(o), source(o)).wait_recv()
    for kind in range(2):
        result[2 + kind] = (own_in[kind].astype(F32) + next_in[kind].astype(F32)).astype(BF16)
        stores[2 + kind].start()
    if fused:
        total = level_acc[g]
        for o in range(1, groups):
            level_copy(o, level_source(o)).wait_recv()
            total = total + level_in[level_source(o)].astype(F32)
        wresult[...] = total
    stores[5].start()

    @pl.when(has_next)
    def _():
        for kind in range(2):
            for o in range(HEADS):
                nxt_copy(kind, o, p).wait_send()

    @pl.when(has_prev)
    def _():
        for kind in range(2):
            for o in range(HEADS):
                prv_copy(kind, peer(o), p).wait_send()

    for o in range(1, HEADS):
        for kind in range(3):
            qkv_copy(kind, o, p).wait_send()
        mix_copy(o, peer(o), p).wait_send()
        dm_copy(o, p).wait_send()
        dq_copy(peer(o), peer(o), p).wait_send()
        for kind in range(2):
            own_copy(kind, peer(o), peer(o), p).wait_send()
    if fused:
        pair_copy.wait_send()
        for o in range(1, chips):
            chip_copy(o, chip).wait_send()
        for o in range(1, groups):
            level_copy(o, g).wait_send()
    for store in stores:
        store.wait()


def shards(queries, keys, values, gates, cotangent, segment, w_out):
    rows, features = queries.shape[1:]
    hd = features // HEADS
    span = HEADS * rows
    chips = HEADS // 2
    groups = lax.axis_size("seq") // HEADS
    g = lax.axis_index("seq") // HEADS
    copies = lax.axis_size("dp") * groups * HEADS
    share = features // copies
    fused = lax.axis_size("dp") == 1 and share % 16 == 0
    kept = share if fused else 16
    wrows = share if fused else features
    anywhere = pl.BlockSpec(memory_space=pl.ANY)
    vm = pl.BlockSpec(memory_space=pltpu.VMEM)
    token = jax.ShapeDtypeStruct((rows, features), BF16)
    dma = pltpu.SemaphoreType.DMA
    results = pl.pallas_call(
        functools.partial(kernel, groups, fused),
        out_shape=(token,) * 5 + (jax.ShapeDtypeStruct((wrows, features), F32),),
        in_specs=[anywhere] * 6 + [vm],
        out_specs=(anywhere,) * 6,
        scratch_shapes=[
            pltpu.VMEM((rows, features), BF16),
            pltpu.VMEM((rows, features), BF16),
            pltpu.VMEM((features, features), BF16),
            pltpu.VMEM((5, rows, features), BF16),
            pltpu.VMEM((wrows, features), F32),
            pltpu.VMEM((1, 2 * span), jnp.int32),
            pltpu.VMEM((span, hd), BF16),
            pltpu.VMEM((2 * span, hd), BF16),
            pltpu.VMEM((2 * span, hd), BF16),
            pltpu.VMEM((span, span + rows), BF16),
            pltpu.VMEM((span, span + rows), F32),
            pltpu.VMEM((span, hd), F32),
            pltpu.VMEM((rows, features), F32),
            pltpu.VMEM((rows, features), F32),
            pltpu.VMEM((rows, features), BF16),
            pltpu.VMEM((rows, features), BF16),
            pltpu.VMEM((span, hd), BF16),
            pltpu.VMEM((span, hd), BF16),
            pltpu.VMEM((2 * span, hd), F32),
            pltpu.VMEM((2 * span, hd), F32),
            pltpu.VMEM((2 * span, hd), BF16),
            pltpu.VMEM((2 * span, hd), BF16),
            pltpu.VMEM((rows, features), BF16),
            pltpu.VMEM((2, rows, features), BF16),
            pltpu.VMEM((2, rows, features), BF16),
            pltpu.VMEM((2, chips, groups, kept, features), F32),
            pltpu.VMEM((2, chips, groups, kept, features), BF16),
            pltpu.VMEM((chips, groups, kept, features), BF16),
            pltpu.VMEM((groups, kept, features), F32),
            pltpu.VMEM((chips, groups, kept, features), BF16),
            pltpu.VMEM((chips, groups, kept, features), BF16),
            pltpu.VMEM((groups, kept, features), F32),
            pltpu.VMEM((groups, kept, features), BF16),
            pltpu.VMEM((groups, kept, features), BF16),
            dma((3, HEADS)), dma((3, HEADS)),
            dma((2, HEADS)), dma((2, HEADS)),
            dma((HEADS,)), dma((HEADS,)),
            dma((HEADS,)), dma((HEADS,)),
            dma((HEADS,)), dma((HEADS,)),
            dma((2, HEADS)), dma((2, HEADS)),
            dma((2, HEADS)), dma((2, HEADS)),
            dma, dma,
            dma((chips,)), dma((chips,)),
            dma((groups,)), dma((groups,)),
            dma((6,)), dma((6,)),
        ],
        compiler_params=pltpu.CompilerParams(
            collective_id=0, has_side_effects=True, vmem_limit_bytes=48 * 1024 * 1024
        ),
        cost_estimate=pl.CostEstimate(
            flops=3_000_000_000, bytes_accessed=12_000_000, transcendentals=1_200_000
        ),
    )(
        queries[0], keys[0], values[0], gates[0], cotangent[0], w_out, segment,
    )
    output, dq, dk, dv, dgate, weight_grad = results
    if not fused:
        weight_grad = lax.psum_scatter(weight_grad, ("dp", "seq"), scatter_dimension=0, tiled=True)
    return output[None], dq[None], dk[None], dv[None], dgate[None], weight_grad


def solution(mesh):
    tokens = P("dp", "seq", None)
    return jax.shard_map(
        shards,
        mesh=mesh,
        in_specs=(tokens,) * 5 + (P("dp", None), P()),
        out_specs=(tokens,) * 5 + (P(("dp", "seq"), None),),
        check_vma=False,
    )
```

```python
import functools
import math

import jax
import jax.numpy as jnp
from jax import lax
from jax.experimental import pallas as pl
from jax.experimental.pallas import tpu as pltpu
from jax.sharding import PartitionSpec as P

HEADS = 8
EPS = 1e-05
F32 = jnp.float32
BF16 = jnp.bfloat16


def dot_nn(a, b):
    return lax.dot_general(a, b, (((1,), (0,)), ((), ())), preferred_element_type=F32)


def dot_nt(a, b):
    return lax.dot_general(a, b, (((1,), (1,)), ((), ())), preferred_element_type=F32)


def dot_tn(a, b):
    return lax.dot_general(a, b, (((0,), (0,)), ((), ())), preferred_element_type=F32)


def kernel(
    groups, fused,
    q_ref, k_ref, v_ref, gate_hbm, cot_hbm, w_hbm, seg_ref,
    out_ref, dq_ref, dk_ref, dv_ref, dgate_ref, wgrad_ref,
    gate_ref, cot_ref, w_ref, result, wresult, seg_win, seg_col,
    qh, kh, vh, k_turned, v_turned, wts, slope, mix_part, mix_stage, mix_in, dgated, gated,
    dmix_stage, dmh, dq_part, dq_stage, dk_acc, dv_acc, dk_stage, dv_stage, dq_in, own_in, next_in,
    part, part_send, pair_in, chip_acc, chip_send, chip_in, level_acc, level_send, level_in,
    s_qkv, r_qkv, s_nxt, r_nxt, s_mix, r_mix, s_dm, r_dm, s_dq, r_dq, s_own, r_own, s_prv, r_prv,
    s_pair, r_pair, s_chip, r_chip, s_level, r_level, s_load, s_store,
):
    rows = q_ref.shape[0]
    features = q_ref.shape[1]
    hd = features // HEADS
    span = HEADS * rows
    wide = 2 * rows
    scale = 1.0 / math.sqrt(hd)
    me = lax.axis_index("seq")
    g = me // HEADS
    p = lax.rem(me, HEADS)
    base = g * HEADS
    has_prev = g > 0
    has_next = g < groups - 1
    core = lax.rem(p, 2)
    chip = p // 2
    chips = HEADS // 2

    def rs(i):
        return pl.ds(pl.multiple_of(i * rows, rows), rows)

    def cs(i):
        return pl.ds(pl.multiple_of(i * hd, hd), hd)

    def peer(o):
        return lax.rem(p + o, HEADS)

    def source(o):
        return lax.rem(p + HEADS - o, HEADS)

    def copy(src, dst, ss, rsem, dev):
        return pltpu.make_async_remote_copy(
            src_ref=src, dst_ref=dst, send_sem=ss, recv_sem=rsem,
            device_id={"seq": dev}, device_id_type=pl.DeviceIdType.MESH,
        )

    barrier = pltpu.get_barrier_semaphore()

    def greet(dev):
        pl.semaphore_signal(
            barrier, inc=1, device_id={"seq": dev}, device_id_type=pl.DeviceIdType.MESH
        )

    for o in range(1, HEADS):
        greet(base + peer(o))

    def level(o):
        return lax.rem(g + o, groups)

    def level_source(o):
        return lax.rem(g + groups - o, groups)

    for o in range(1, groups):
        greet(level(o) * HEADS + p)
    loads = [
        pltpu.make_async_copy(src, dst, s_load.at[i])
        for i, (src, dst) in enumerate(
            (
                (cot_hbm, cot_ref), (w_hbm, w_ref), (gate_hbm, gate_ref),
                (k_ref.at[:, cs(p)], kh.at[rs(HEADS + p)]),
                (v_ref.at[:, cs(p)], vh.at[rs(HEADS + p)]),
                (q_ref.at[:, cs(p)], qh.at[rs(p)]),
            )
        )
    ]
    for load in loads:
        load.start()
    pl.semaphore_wait(barrier, HEADS + groups - 2)

    ins = ((k_ref, kh, HEADS), (v_ref, vh, HEADS), (q_ref, qh, 0))

    def qkv_copy(kind, o, where):
        src, dst, off = ins[kind]
        return copy(src.at[:, cs(peer(o))], dst.at[rs(off + where)],
                    s_qkv.at[kind, o], r_qkv.at[kind, o], base + peer(o))

    def nxt_copy(kind, o):
        src, dst, off = ins[kind]
        at = source(o)
        held = src.at[:, cs(p)] if o == 0 else dst.at[rs(off + at)]
        return copy(held, dst.at[rs(at)], s_nxt.at[kind, at], r_nxt.at[kind, at],
                    base + HEADS + p)

    @pl.when(has_next)
    def _():
        for kind in range(2):
            nxt_copy(kind, 0).start()

    for o in range(1, HEADS):
        for kind in range(2):
            qkv_copy(kind, o, p).start()
    for o in range(1, HEADS):
        qkv_copy(2, o, p).start()
    seg_own = seg_ref[:, pl.ds(pl.multiple_of(g * span, span), span)]
    seg_before = seg_ref[:, pl.ds(pl.multiple_of(jnp.maximum(g - 1, 0) * span, span), span)]
    seg_win[:, pl.ds(span, span)] = seg_own
    seg_win[:, pl.ds(0, span)] = jnp.where(has_prev, seg_before, -1)

    @pl.when(jnp.logical_not(has_prev))
    def _():
        kh[pl.ds(0, span), :] = jnp.zeros((span, hd), BF16)
        vh[pl.ds(0, span), :] = jnp.zeros((span, hd), BF16)

    def seg_block(j, carry):
        line = seg_win[:, rs(j)]
        seg_col[rs(j), :] = jnp.transpose(jnp.broadcast_to(line, (rows, rows)))
        return carry

    lax.fori_loop(0, 2 * HEADS, seg_block, 0)
    dk_acc[...] = jnp.zeros_like(dk_acc)
    dv_acc[...] = jnp.zeros_like(dv_acc)
    for o in range(1, HEADS):
        for kind in range(2):
            qkv_copy(kind, o, source(o)).wait_recv()

            @pl.when(has_next)
            def _():
                nxt_copy(kind, o).start()

    for load in loads:
        load.wait()
    dgated[...] = dot_nt(cot_ref[...], w_ref[...])
    for ref, turned in ((kh, k_turned), (vh, v_turned)):
        turned[:, pl.ds(span, span)] = jnp.transpose(ref[pl.ds(span, span), :])
    for o in range(1, HEADS):
        qkv_copy(2, o, source(o)).wait_recv()

    def bounds(i, own):
        lo = span if own else i * wide
        hi = span + (i + 1) * wide if own else span
        return lo, hi, slice(lo - i * wide, hi - i * wide), slice(i * wide, (i + 1) * wide)

    def forward(i, own):
        lo, hi, held, mine = bounds(i, own)
        scores = dot_nt(kh[lo:hi, :], qh[mine, :]) * scale
        seg_k = seg_col[lo:hi, :]
        seg_q = seg_win[:, span + i * wide : span + (i + 1) * wide]
        allowed = jnp.concatenate([seg_k, seg_k], axis=1) == seg_q
        if own:
            kj = lax.broadcasted_iota(jnp.int32, scores.shape, 0)
            qi = lax.broadcasted_iota(jnp.int32, scores.shape, 1)
            allowed = allowed & (kj - i * wide <= qi)
        sig = 1.0 / (1.0 + jnp.exp(-jnp.maximum(scores, -80.0)))
        sig = jnp.where(allowed, sig, 0.0)
        silu = scores * sig
        w = silu.astype(BF16)
        wts[i, held, :] = w
        slope[i, held, :] = (sig + silu * (1.0 - sig)) * scale
        return dot_nn(v_turned[:, lo:hi], w)

    def mix_copy(t, dev, col):
        return copy(mix_stage.at[rs(t)], mix_in.at[:, cs(col)],
                    s_mix.at[t], r_mix.at[col], base + dev)

    for i in range(chips):
        mix_part[i] = forward(i, True)

    @pl.when(has_prev)
    def _():
        for o in range(HEADS):
            for kind in range(2):
                nxt_copy(kind, o).wait_recv()

    for ref, turned in ((kh, k_turned), (vh, v_turned)):
        turned[:, pl.ds(0, span)] = jnp.transpose(ref[pl.ds(0, span), :])

    def finish(o, carry):
        now = lax.rem(chip + 1 + o, chips)
        for i in range(chips):

            @pl.when(now == i)
            def _():
                mixed = mix_part[i] + forward(i, False)
                mix_stage[i * wide : (i + 1) * wide, :] = jnp.transpose(mixed)
                for t in (2 * i, 2 * i + 1):

                    @pl.when(t != p)
                    def _():
                        mix_copy(t, t, p).start()

        return carry

    lax.fori_loop(0, chips, finish, 0)
    mix_in[:, cs(p)] = mix_stage[rs(p), :]
    for o in range(1, HEADS):
        mix_copy(p, p, source(o)).wait_recv()

    mixed = mix_in[...]
    centred = mixed - jnp.mean(mixed, axis=-1, keepdims=True)
    inverse = lax.rsqrt(jnp.mean(centred * centred, axis=-1, keepdims=True) + EPS)
    normed = centred * inverse
    gate = gate_ref[...].astype(F32)
    dg = dgated[...]
    dnormed = dg * gate
    dmixed = inverse * (
        dnormed
        - jnp.mean(dnormed, axis=-1, keepdims=True)
        - normed * jnp.mean(dnormed * normed, axis=-1, keepdims=True)
    )
    dmix_stage[...] = dmixed.astype(BF16)

    def dm_copy(o, where):
        return copy(dmix_stage.at[:, cs(peer(o))], dmh.at[rs(where)],
                    s_dm.at[o], r_dm.at[o], base + peer(o))

    for o in range(1, HEADS):
        dm_copy(o, p).start()
    dmh[rs(p), :] = dmix_stage[:, cs(p)]
    gated[...] = (normed * gate).astype(BF16)
    def chip_copy(o, where):
        there = lax.rem(chip + o, chips)
        return copy(chip_send.at[there], chip_in.at[where],
                    s_chip.at[o], r_chip.at[o], base + 2 * there + core)

    def level_copy(o, where):
        return copy(level_send.at[level(o)], level_in.at[where],
                    s_level.at[o], r_level.at[o], level(o) * HEADS + p)

    if fused:
        pair_copy = copy(part_send.at[1 - core], pair_in, s_pair, r_pair, base + p + 1 - 2 * core)
        share = part.shape[3]
        block = HEADS * share
        for i in range(groups):
            product = dot_tn(gated[:, i * block : (i + 1) * block], cot_ref[...])
            for j in range(HEADS):
                piece = product[j * share : (j + 1) * share]
                part[j % 2, j // 2, i] = piece
                part_send[j % 2, j // 2, i] = piece.astype(BF16)
        pair_copy.start()
    else:

        def weight_chunk(c, carry):
            wresult[rs(c), :] = dot_tn(gated[:, cs(c)], cot_ref[...])
            return carry

        lax.fori_loop(0, HEADS, weight_chunk, 0)
    result[1] = (dg * normed).astype(BF16)
    result[0] = dot_nn(gated[...], w_ref[...]).astype(BF16)
    outs = (out_ref, dq_ref, dk_ref, dv_ref, dgate_ref)
    ready = (result.at[0], dq_in, own_in.at[0], own_in.at[1], result.at[1])
    stores = [
        pltpu.make_async_copy(src, ref, s_store.at[i])
        for i, (src, ref) in enumerate(zip(ready, outs))
    ]
    stores.append(pltpu.make_async_copy(wresult, wgrad_ref, s_store.at[5]))
    stores[0].start()
    stores[4].start()
    if fused:
        pair_copy.wait_recv()
        for o in range(1, chips):
            there = lax.rem(chip + o, chips)
            chip_send[there] = (part[core, there] + pair_in[there].astype(F32)).astype(BF16)
            chip_copy(o, chip).start()
        chip_acc[...] = part[core, chip] + pair_in[chip].astype(F32)
    for o in range(1, HEADS):
        dm_copy(o, source(o)).wait_recv()

    grads = ((dk_acc, dk_stage), (dv_acc, dv_stage))

    def dq_copy(b, dev, col):
        return copy(dq_stage.at[rs(b)], dq_in.at[:, cs(col)], s_dq.at[b], r_dq.at[col], base + dev)

    def prv_copy(kind, i):
        held = pl.ds(i * wide, wide)
        return copy(grads[kind][1].at[held], next_in.at[kind, held],
                    s_prv.at[kind, i], r_prv.at[kind, i], base - HEADS + p)

    def own_copy(kind, b, dev, col):
        return copy(grads[kind][1].at[rs(HEADS + b)], own_in.at[kind, :, cs(col)],
                    s_own.at[kind, b], r_own.at[kind, col], base + dev)

    def backward(i, own):
        lo, hi, held, mine = bounds(i, own)
        dm = dmh[mine, :]
        ds = (dot_nt(vh[lo:hi, :], dm) * slope[i, held, :]).astype(BF16)
        dk_acc[lo:hi, :] += dot_nn(ds, qh[mine, :])
        dv_acc[lo:hi, :] += dot_nn(wts[i, held, :], dm)
        return dot_nn(k_turned[:, lo:hi], ds)

    for i in range(chips):
        dq_part[i] = backward(i, False)
        held = pl.ds(i * wide, wide)
        for acc, stage in grads:
            stage[held, :] = acc[held, :].astype(BF16)

        @pl.when(has_prev)
        def _():
            for kind in range(2):
                prv_copy(kind, i).start()

    for i in range(chips):
        dq = dq_part[i] + backward(i, True)
        dq_stage[i * wide : (i + 1) * wide, :] = jnp.transpose(dq).astype(BF16)
    for o in range(1, HEADS):
        dq_copy(peer(o), peer(o), p).start()
    dq_in[:, cs(p)] = dq_stage[rs(p), :]

    @pl.when(jnp.logical_not(has_next))
    def _():
        next_in[...] = jnp.zeros_like(next_in)

    @pl.when(has_next)
    def _():
        for i in range(chips):
            for kind in range(2):
                prv_copy(kind, i).wait_recv()

    for kind, (acc, stage) in enumerate(grads):
        both = acc[pl.ds(span, span), :] + next_in[kind].astype(F32)
        stage[pl.ds(span, span), :] = both.astype(BF16)
    for o in range(1, HEADS):
        for kind in range(2):
            own_copy(kind, peer(o), peer(o), p).start()
    for kind in range(2):
        own_in[kind, :, cs(p)] = grads[kind][1][rs(HEADS + p), :]
    if fused:
        total = chip_acc[...]
        for o in range(1, chips):
            there = lax.rem(chip + chips - o, chips)
            chip_copy(o, there).wait_recv()
            total = total + chip_in[there].astype(F32)
        level_acc[...] = total
        level_send[...] = total.astype(BF16)
        for o in range(1, groups):
            level_copy(o, g).start()

    for o in range(1, HEADS):
        dq_copy(peer(o), peer(o), source(o)).wait_recv()
    stores[1].start()

    for kind in range(2):
        for o in range(1, HEADS):
            own_copy(kind, peer(o), peer(o), source(o)).wait_recv()
    for kind in range(2):
        stores[2 + kind].start()
    if fused:
        total = level_acc[g]
        for o in range(1, groups):
            level_copy(o, level_source(o)).wait_recv()
            total = total + level_in[level_source(o)].astype(F32)
        wresult[...] = total
    stores[5].start()

    @pl.when(has_next)
    def _():
        for kind in range(2):
            for o in range(HEADS):
                nxt_copy(kind, o).wait_send()

    @pl.when(has_prev)
    def _():
        for kind in range(2):
            for i in range(chips):
                prv_copy(kind, i).wait_send()

    for o in range(1, HEADS):
        for kind in range(3):
            qkv_copy(kind, o, p).wait_send()
        mix_copy(peer(o), peer(o), p).wait_send()
        dm_copy(o, p).wait_send()
        dq_copy(peer(o), peer(o), p).wait_send()
        for kind in range(2):
            own_copy(kind, peer(o), peer(o), p).wait_send()
    if fused:
        pair_copy.wait_send()
        for o in range(1, chips):
            chip_copy(o, chip).wait_send()
        for o in range(1, groups):
            level_copy(o, g).wait_send()
    for store in stores:
        store.wait()


def shards(queries, keys, values, gates, cotangent, segment, w_out):
    rows, features = queries.shape[1:]
    hd = features // HEADS
    span = HEADS * rows
    chips = HEADS // 2
    groups = lax.axis_size("seq") // HEADS
    g = lax.axis_index("seq") // HEADS
    copies = lax.axis_size("dp") * groups * HEADS
    share = features // copies
    fused = lax.axis_size("dp") == 1 and share % 16 == 0
    kept = share if fused else 16
    wrows = share if fused else features
    anywhere = pl.BlockSpec(memory_space=pl.ANY)
    vm = pl.BlockSpec(memory_space=pltpu.VMEM)
    token = jax.ShapeDtypeStruct((rows, features), BF16)
    dma = pltpu.SemaphoreType.DMA
    results = pl.pallas_call(
        functools.partial(kernel, groups, fused),
        out_shape=(token,) * 5 + (jax.ShapeDtypeStruct((wrows, features), F32),),
        in_specs=[anywhere] * 6 + [vm],
        out_specs=(anywhere,) * 6,
        scratch_shapes=[
            pltpu.VMEM((rows, features), BF16),
            pltpu.VMEM((rows, features), BF16),
            pltpu.VMEM((features, features), BF16),
            pltpu.VMEM((2, rows, features), BF16),
            pltpu.VMEM((wrows, features), F32),
            pltpu.VMEM((1, 2 * span), jnp.int32),
            pltpu.VMEM((2 * span, rows), jnp.int32),
            pltpu.VMEM((span, hd), BF16),
            pltpu.VMEM((2 * span, hd), BF16),
            pltpu.VMEM((2 * span, hd), BF16),
            pltpu.VMEM((hd, 2 * span), BF16),
            pltpu.VMEM((hd, 2 * span), BF16),
            pltpu.VMEM((chips, span + 2 * rows, 2 * rows), BF16),
            pltpu.VMEM((chips, span + 2 * rows, 2 * rows), F32),
            pltpu.VMEM((chips, hd, 2 * rows), F32),
            pltpu.VMEM((span, hd), F32),
            pltpu.VMEM((rows, features), F32),
            pltpu.VMEM((rows, features), F32),
            pltpu.VMEM((rows, features), BF16),
            pltpu.VMEM((rows, features), BF16),
            pltpu.VMEM((span, hd), BF16),
            pltpu.VMEM((chips, hd, 2 * rows), F32),
            pltpu.VMEM((span, hd), BF16),
            pltpu.VMEM((2 * span, hd), F32),
            pltpu.VMEM((2 * span, hd), F32),
            pltpu.VMEM((2 * span, hd), BF16),
            pltpu.VMEM((2 * span, hd), BF16),
            pltpu.VMEM((rows, features), BF16),
            pltpu.VMEM((2, rows, features), BF16),
            pltpu.VMEM((2, span, hd), BF16),
            pltpu.VMEM((2, chips, groups, kept, features), F32),
            pltpu.VMEM((2, chips, groups, kept, features), BF16),
            pltpu.VMEM((chips, groups, kept, features), BF16),
            pltpu.VMEM((groups, kept, features), F32),
            pltpu.VMEM((chips, groups, kept, features), BF16),
            pltpu.VMEM((chips, groups, kept, features), BF16),
            pltpu.VMEM((groups, kept, features), F32),
            pltpu.VMEM((groups, kept, features), BF16),
            pltpu.VMEM((groups, kept, features), BF16),
            dma((3, HEADS)), dma((3, HEADS)),
            dma((2, HEADS)), dma((2, HEADS)),
            dma((HEADS,)), dma((HEADS,)),
            dma((HEADS,)), dma((HEADS,)),
            dma((HEADS,)), dma((HEADS,)),
            dma((2, HEADS)), dma((2, HEADS)),
            dma((2, chips)), dma((2, chips)),
            dma, dma,
            dma((chips,)), dma((chips,)),
            dma((groups,)), dma((groups,)),
            dma((6,)), dma((6,)),
        ],
        compiler_params=pltpu.CompilerParams(
            collective_id=0, has_side_effects=True, vmem_limit_bytes=62 * 1024 * 1024
        ),
        cost_estimate=pl.CostEstimate(
            flops=3_000_000_000, bytes_accessed=12_000_000, transcendentals=1_200_000
        ),
    )(
        queries[0], keys[0], values[0], gates[0], cotangent[0], w_out, segment,
    )
    output, dq, dk, dv, dgate, weight_grad = results
    if not fused:
        weight_grad = lax.psum_scatter(weight_grad, ("dp", "seq"), scatter_dimension=0, tiled=True)
    return output[None], dq[None], dk[None], dv[None], dgate[None], weight_grad


def solution(mesh):
    tokens = P("dp", "seq", None)
    return jax.shard_map(
        shards,
        mesh=mesh,
        in_specs=(tokens,) * 5 + (P("dp", None), P()),
        out_specs=(tokens,) * 5 + (P(("dp", "seq"), None),),
        check_vma=False,
    )
```

```python
import functools
import math

import jax
import jax.numpy as jnp
from jax import lax
from jax.experimental import pallas as pl
from jax.experimental.pallas import tpu as pltpu
from jax.sharding import PartitionSpec as P

HEADS = 8
EPS = 1e-05
F32 = jnp.float32
BF16 = jnp.bfloat16


def dot_nn(a, b):
    return lax.dot_general(a, b, (((1,), (0,)), ((), ())), preferred_element_type=F32)


def dot_nt(a, b):
    return lax.dot_general(a, b, (((1,), (1,)), ((), ())), preferred_element_type=F32)


def dot_tn(a, b):
    return lax.dot_general(a, b, (((0,), (0,)), ((), ())), preferred_element_type=F32)


def kernel(
    groups, fused,
    q_ref, k_ref, v_ref, gate_hbm, cot_hbm, w_hbm, seg_ref,
    out_ref, dq_ref, dk_ref, dv_ref, dgate_ref, wgrad_ref,
    gate_ref, cot_ref, w_ref, result, wresult, seg_win, seg_col,
    qh, kh, vh, k_turned, v_turned, wts, slope, mix_part, mix_stage, mix_in, dgated, gated,
    dmix_stage, dmh, dq_part, dq_stage, dk_acc, dv_acc, dk_stage, dv_stage, dq_in, own_in, next_in,
    part, part_send, pair_in, chip_acc, chip_send, chip_in, level_acc, level_send, level_in,
    s_qkv, r_qkv, s_nxt, r_nxt, s_mix, r_mix, s_dm, r_dm, s_dq, r_dq, s_own, r_own, s_prv, r_prv,
    s_pair, r_pair, s_chip, r_chip, s_level, r_level, s_load, s_store,
):
    rows = q_ref.shape[0]
    features = q_ref.shape[1]
    hd = features // HEADS
    span = HEADS * rows
    wide = 2 * rows
    scale = 1.0 / math.sqrt(hd)
    me = lax.axis_index("seq")
    g = me // HEADS
    p = lax.rem(me, HEADS)
    base = g * HEADS
    has_prev = g > 0
    has_next = g < groups - 1
    core = lax.rem(p, 2)
    chip = p // 2
    chips = HEADS // 2

    def rs(i):
        return pl.ds(pl.multiple_of(i * rows, rows), rows)

    def cs(i):
        return pl.ds(pl.multiple_of(i * hd, hd), hd)

    def peer(o):
        return lax.rem(p + o, HEADS)

    def source(o):
        return lax.rem(p + HEADS - o, HEADS)

    def copy(src, dst, ss, rsem, dev):
        return pltpu.make_async_remote_copy(
            src_ref=src, dst_ref=dst, send_sem=ss, recv_sem=rsem,
            device_id={"seq": dev}, device_id_type=pl.DeviceIdType.MESH,
        )

    barrier = pltpu.get_barrier_semaphore()

    def greet(dev):
        pl.semaphore_signal(
            barrier, inc=1, device_id={"seq": dev}, device_id_type=pl.DeviceIdType.MESH
        )

    for o in range(1, HEADS):
        greet(base + peer(o))

    def level(o):
        return lax.rem(g + o, groups)

    def level_source(o):
        return lax.rem(g + groups - o, groups)

    for o in range(1, groups):
        greet(level(o) * HEADS + p)
    loads = [
        pltpu.make_async_copy(src, dst, s_load.at[i])
        for i, (src, dst) in enumerate(
            (
                (cot_hbm, cot_ref), (w_hbm, w_ref), (gate_hbm, gate_ref),
                (k_ref.at[:, cs(p)], kh.at[rs(HEADS + p)]),
                (v_ref.at[:, cs(p)], vh.at[rs(HEADS + p)]),
                (q_ref.at[:, cs(p)], qh.at[rs(p)]),
            )
        )
    ]
    for load in loads:
        load.start()
    pl.semaphore_wait(barrier, HEADS + groups - 2)

    ins = ((k_ref, kh, HEADS), (v_ref, vh, HEADS), (q_ref, qh, 0))

    def qkv_copy(kind, o, where):
        src, dst, off = ins[kind]
        return copy(src.at[:, cs(peer(o))], dst.at[rs(off + where)],
                    s_qkv.at[kind, o], r_qkv.at[kind, o], base + peer(o))

    def nxt_copy(kind, o):
        src, dst, off = ins[kind]
        at = source(o)
        held = src.at[:, cs(p)] if o == 0 else dst.at[rs(off + at)]
        return copy(held, dst.at[rs(at)], s_nxt.at[kind, at], r_nxt.at[kind, at],
                    base + HEADS + p)

    @pl.when(has_next)
    def _():
        for kind in range(2):
            nxt_copy(kind, 0).start()

    for o in range(1, HEADS):
        for kind in range(2):
            qkv_copy(kind, o, p).start()
    for o in range(1, HEADS):
        qkv_copy(2, o, p).start()
    seg_own = seg_ref[:, pl.ds(pl.multiple_of(g * span, span), span)]
    seg_before = seg_ref[:, pl.ds(pl.multiple_of(jnp.maximum(g - 1, 0) * span, span), span)]
    seg_win[:, pl.ds(span, span)] = seg_own
    seg_win[:, pl.ds(0, span)] = jnp.where(has_prev, seg_before, -1)

    @pl.when(jnp.logical_not(has_prev))
    def _():
        kh[pl.ds(0, span), :] = jnp.zeros((span, hd), BF16)
        vh[pl.ds(0, span), :] = jnp.zeros((span, hd), BF16)

    def seg_block(j, carry):
        line = seg_win[:, rs(j)]
        seg_col[rs(j), :] = jnp.transpose(jnp.broadcast_to(line, (rows, rows)))
        return carry

    lax.fori_loop(0, 2 * HEADS, seg_block, 0)
    dk_acc[...] = jnp.zeros_like(dk_acc)
    dv_acc[...] = jnp.zeros_like(dv_acc)
    for o in range(1, HEADS):
        for kind in range(2):
            qkv_copy(kind, o, source(o)).wait_recv()

            @pl.when(has_next)
            def _():
                nxt_copy(kind, o).start()

    for load in loads:
        load.wait()
    dgated[...] = dot_nt(cot_ref[...], w_ref[...])
    for ref, turned in ((kh, k_turned), (vh, v_turned)):
        turned[:, pl.ds(span, span)] = jnp.transpose(ref[pl.ds(span, span), :])
    for o in range(1, HEADS):
        qkv_copy(2, o, source(o)).wait_recv()

    def bounds(i, own):
        lo = span if own else i * wide
        hi = span + (i + 1) * wide if own else span
        return lo, hi, slice(lo - i * wide, hi - i * wide), slice(i * wide, (i + 1) * wide)

    def forward(i, own):
        lo, hi, held, mine = bounds(i, own)
        scores = dot_nt(kh[lo:hi, :], qh[mine, :]) * scale
        seg_k = seg_col[lo:hi, :]
        seg_q = seg_win[:, span + i * wide : span + (i + 1) * wide]
        allowed = jnp.concatenate([seg_k, seg_k], axis=1) == seg_q
        if own:
            kj = lax.broadcasted_iota(jnp.int32, scores.shape, 0)
            qi = lax.broadcasted_iota(jnp.int32, scores.shape, 1)
            allowed = allowed & (kj - i * wide <= qi)
        sig = 1.0 / (1.0 + jnp.exp(-jnp.maximum(scores, -80.0)))
        sig = jnp.where(allowed, sig, 0.0)
        silu = scores * sig
        w = silu.astype(BF16)
        wts[i, held, :] = w
        slope[i, held, :] = (sig + silu * (1.0 - sig)) * scale
        return dot_nn(v_turned[:, lo:hi], w)

    def mix_copy(t, dev, col):
        return copy(mix_stage.at[rs(t)], mix_in.at[:, cs(col)],
                    s_mix.at[t], r_mix.at[col], base + dev)

    for i in range(chips):
        mix_part[i] = forward(i, True)

    @pl.when(has_prev)
    def _():
        for o in range(HEADS):
            for kind in range(2):
                nxt_copy(kind, o).wait_recv()

    for ref, turned in ((kh, k_turned), (vh, v_turned)):
        turned[:, pl.ds(0, span)] = jnp.transpose(ref[pl.ds(0, span), :])

    def finish(o, carry):
        now = lax.rem(chip + 1 + o, chips)
        for i in range(chips):

            @pl.when(now == i)
            def _():
                mixed = mix_part[i] + forward(i, False)
                mix_stage[i * wide : (i + 1) * wide, :] = jnp.transpose(mixed)
                for t in (2 * i, 2 * i + 1):

                    @pl.when(t != p)
                    def _():
                        mix_copy(t, t, p).start()

        return carry

    lax.fori_loop(0, chips, finish, 0)
    mix_in[:, cs(p)] = mix_stage[rs(p), :]
    for o in range(1, HEADS):
        mix_copy(p, p, source(o)).wait_recv()

    mixed = mix_in[...]
    centred = mixed - jnp.mean(mixed, axis=-1, keepdims=True)
    inverse = lax.rsqrt(jnp.mean(centred * centred, axis=-1, keepdims=True) + EPS)
    normed = centred * inverse
    gate = gate_ref[...].astype(F32)
    dg = dgated[...]
    dnormed = dg * gate
    dmixed = inverse * (
        dnormed
        - jnp.mean(dnormed, axis=-1, keepdims=True)
        - normed * jnp.mean(dnormed * normed, axis=-1, keepdims=True)
    )
    dmix_stage[...] = dmixed.astype(BF16)

    def dm_copy(o, where):
        return copy(dmix_stage.at[:, cs(peer(o))], dmh.at[rs(where)],
                    s_dm.at[o], r_dm.at[o], base + peer(o))

    for o in range(1, HEADS):
        dm_copy(o, p).start()
    dmh[rs(p), :] = dmix_stage[:, cs(p)]
    gated[...] = (normed * gate).astype(BF16)
    def chip_copy(o, where):
        there = lax.rem(chip + o, chips)
        return copy(chip_send.at[there], chip_in.at[where],
                    s_chip.at[o], r_chip.at[o], base + 2 * there + core)

    def level_copy(o, where):
        return copy(level_send.at[level(o)], level_in.at[where],
                    s_level.at[o], r_level.at[o], level(o) * HEADS + p)

    if fused:
        pair_copy = copy(part_send.at[1 - core], pair_in, s_pair, r_pair, base + p + 1 - 2 * core)
        share = part.shape[3]
        block = HEADS * share
        for i in range(groups):
            product = dot_tn(gated[:, i * block : (i + 1) * block], cot_ref[...])
            for j in range(HEADS):
                piece = product[j * share : (j + 1) * share]
                part[j % 2, j // 2, i] = piece
                part_send[j % 2, j // 2, i] = piece.astype(BF16)
        pair_copy.start()
    else:

        def weight_chunk(c, carry):
            wresult[rs(c), :] = dot_tn(gated[:, cs(c)], cot_ref[...])
            return carry

        lax.fori_loop(0, HEADS, weight_chunk, 0)
    result[1] = (dg * normed).astype(BF16)
    result[0] = dot_nn(gated[...], w_ref[...]).astype(BF16)
    outs = (out_ref, dq_ref, dk_ref, dv_ref, dgate_ref)
    ready = (result.at[0], dq_in, own_in.at[0], own_in.at[1], result.at[1])
    stores = [
        pltpu.make_async_copy(src, ref, s_store.at[i])
        for i, (src, ref) in enumerate(zip(ready, outs))
    ]
    stores.append(pltpu.make_async_copy(wresult, wgrad_ref, s_store.at[5]))
    stores[0].start()
    stores[4].start()
    if fused:
        pair_copy.wait_recv()
        for o in range(1, chips):
            there = lax.rem(chip + o, chips)
            chip_send[there] = (part[core, there] + pair_in[there].astype(F32)).astype(BF16)
            chip_copy(o, chip).start()
        chip_acc[...] = part[core, chip] + pair_in[chip].astype(F32)
    for o in range(1, HEADS):
        dm_copy(o, source(o)).wait_recv()

    grads = ((dk_acc, dk_stage), (dv_acc, dv_stage))

    def dq_copy(b, dev, col):
        return copy(dq_stage.at[rs(b)], dq_in.at[:, cs(col)], s_dq.at[b], r_dq.at[col], base + dev)

    def prv_copy(kind, i):
        held = pl.ds(i * wide, wide)
        return copy(grads[kind][1].at[held], next_in.at[kind, held],
                    s_prv.at[kind, i], r_prv.at[kind, i], base - HEADS + p)

    def own_copy(kind, b, dev, col):
        return copy(grads[kind][1].at[rs(HEADS + b)], own_in.at[kind, :, cs(col)],
                    s_own.at[kind, b], r_own.at[kind, col], base + dev)

    def backward(i, own):
        lo, hi, held, mine = bounds(i, own)
        dm = dmh[mine, :]
        ds = (dot_nt(vh[lo:hi, :], dm) * slope[i, held, :]).astype(BF16)
        dk_acc[lo:hi, :] += dot_nn(ds, qh[mine, :])
        dv_acc[lo:hi, :] += dot_nn(wts[i, held, :], dm)
        return dot_nn(k_turned[:, lo:hi], ds)

    for i in range(chips):
        dq_part[i] = backward(i, False)
        held = pl.ds(i * wide, wide)
        for acc, stage in grads:
            stage[held, :] = acc[held, :].astype(BF16)

        @pl.when(has_prev)
        def _():
            for kind in range(2):
                prv_copy(kind, i).start()

    for i in range(chips):
        dq = dq_part[i] + backward(i, True)
        dq_stage[i * wide : (i + 1) * wide, :] = jnp.transpose(dq).astype(BF16)
    for o in range(1, HEADS):
        dq_copy(peer(o), peer(o), p).start()
    dq_in[:, cs(p)] = dq_stage[rs(p), :]

    @pl.when(jnp.logical_not(has_next))
    def _():
        next_in[...] = jnp.zeros_like(next_in)

    @pl.when(has_next)
    def _():
        for i in range(chips):
            for kind in range(2):
                prv_copy(kind, i).wait_recv()

    for kind, (acc, stage) in enumerate(grads):
        both = acc[pl.ds(span, span), :] + next_in[kind].astype(F32)
        stage[pl.ds(span, span), :] = both.astype(BF16)
    for o in range(1, HEADS):
        for kind in range(2):
            own_copy(kind, peer(o), peer(o), p).start()
    for kind in range(2):
        own_in[kind, :, cs(p)] = grads[kind][1][rs(HEADS + p), :]
    if fused:
        total = chip_acc[...]
        for o in range(1, chips):
            there = lax.rem(chip + chips - o, chips)
            chip_copy(o, there).wait_recv()
            total = total + chip_in[there].astype(F32)
        level_acc[...] = total
        level_send[...] = total.astype(BF16)
        for o in range(1, groups):
            level_copy(o, g).start()

    for o in range(1, HEADS):
        dq_copy(peer(o), peer(o), source(o)).wait_recv()
    stores[1].start()

    for kind in range(2):
        for o in range(1, HEADS):
            own_copy(kind, peer(o), peer(o), source(o)).wait_recv()
    for kind in range(2):
        stores[2 + kind].start()
    if fused:
        total = level_acc[g]
        for o in range(1, groups):
            level_copy(o, level_source(o)).wait_recv()
            total = total + level_in[level_source(o)].astype(F32)
        wresult[...] = total
    stores[5].start()

    @pl.when(has_next)
    def _():
        for kind in range(2):
            for o in range(HEADS):
                nxt_copy(kind, o).wait_send()

    @pl.when(has_prev)
    def _():
        for kind in range(2):
            for i in range(chips):
                prv_copy(kind, i).wait_send()

    for o in range(1, HEADS):
        for kind in range(3):
            qkv_copy(kind, o, p).wait_send()
        mix_copy(peer(o), peer(o), p).wait_send()
        dm_copy(o, p).wait_send()
        dq_copy(peer(o), peer(o), p).wait_send()
        for kind in range(2):
            own_copy(kind, peer(o), peer(o), p).wait_send()
    if fused:
        pair_copy.wait_send()
        for o in range(1, chips):
            chip_copy(o, chip).wait_send()
        for o in range(1, groups):
            level_copy(o, g).wait_send()
    for store in stores:
        store.wait()


def hand_over(*refs):
    count = len(refs) // 2
    done = refs[-1]
    copies = [
        pltpu.make_async_copy(src, dst, done.at[i])
        for i, (src, dst) in enumerate(zip(refs[:count], refs[count : 2 * count]))
    ]
    for copy in copies:
        copy.start()
    for copy in copies:
        copy.wait()


def shards(queries, keys, values, gates, cotangent, segment, w_out):
    rows, features = queries.shape[1:]
    hd = features // HEADS
    span = HEADS * rows
    chips = HEADS // 2
    groups = lax.axis_size("seq") // HEADS
    g = lax.axis_index("seq") // HEADS
    copies = lax.axis_size("dp") * groups * HEADS
    share = features // copies
    fused = lax.axis_size("dp") == 1 and share % 16 == 0
    kept = share if fused else 16
    wrows = share if fused else features
    anywhere = pl.BlockSpec(memory_space=pl.ANY)
    vm = pl.BlockSpec(memory_space=pltpu.VMEM)
    token = jax.ShapeDtypeStruct((rows, features), BF16)
    dma = pltpu.SemaphoreType.DMA
    results = pl.pallas_call(
        functools.partial(kernel, groups, fused),
        out_shape=(token,) * 5 + (jax.ShapeDtypeStruct((wrows, features), F32),),
        in_specs=[anywhere] * 6 + [vm],
        out_specs=(anywhere,) * 6,
        scratch_shapes=[
            pltpu.VMEM((rows, features), BF16),
            pltpu.VMEM((rows, features), BF16),
            pltpu.VMEM((features, features), BF16),
            pltpu.VMEM((2, rows, features), BF16),
            pltpu.VMEM((wrows, features), F32),
            pltpu.VMEM((1, 2 * span), jnp.int32),
            pltpu.VMEM((2 * span, rows), jnp.int32),
            pltpu.VMEM((span, hd), BF16),
            pltpu.VMEM((2 * span, hd), BF16),
            pltpu.VMEM((2 * span, hd), BF16),
            pltpu.VMEM((hd, 2 * span), BF16),
            pltpu.VMEM((hd, 2 * span), BF16),
            pltpu.VMEM((chips, span + 2 * rows, 2 * rows), BF16),
            pltpu.VMEM((chips, span + 2 * rows, 2 * rows), F32),
            pltpu.VMEM((chips, hd, 2 * rows), F32),
            pltpu.VMEM((span, hd), F32),
            pltpu.VMEM((rows, features), F32),
            pltpu.VMEM((rows, features), F32),
            pltpu.VMEM((rows, features), BF16),
            pltpu.VMEM((rows, features), BF16),
            pltpu.VMEM((span, hd), BF16),
            pltpu.VMEM((chips, hd, 2 * rows), F32),
            pltpu.VMEM((span, hd), BF16),
            pltpu.VMEM((2 * span, hd), F32),
            pltpu.VMEM((2 * span, hd), F32),
            pltpu.VMEM((2 * span, hd), BF16),
            pltpu.VMEM((2 * span, hd), BF16),
            pltpu.VMEM((rows, features), BF16),
            pltpu.VMEM((2, rows, features), BF16),
            pltpu.VMEM((2, span, hd), BF16),
            pltpu.VMEM((2, chips, groups, kept, features), F32),
            pltpu.VMEM((2, chips, groups, kept, features), BF16),
            pltpu.VMEM((chips, groups, kept, features), BF16),
            pltpu.VMEM((groups, kept, features), F32),
            pltpu.VMEM((chips, groups, kept, features), BF16),
            pltpu.VMEM((chips, groups, kept, features), BF16),
            pltpu.VMEM((groups, kept, features), F32),
            pltpu.VMEM((groups, kept, features), BF16),
            pltpu.VMEM((groups, kept, features), BF16),
            dma((3, HEADS)), dma((3, HEADS)),
            dma((2, HEADS)), dma((2, HEADS)),
            dma((HEADS,)), dma((HEADS,)),
            dma((HEADS,)), dma((HEADS,)),
            dma((HEADS,)), dma((HEADS,)),
            dma((2, HEADS)), dma((2, HEADS)),
            dma((2, chips)), dma((2, chips)),
            dma, dma,
            dma((chips,)), dma((chips,)),
            dma((groups,)), dma((groups,)),
            dma((6,)), dma((6,)),
        ],
        compiler_params=pltpu.CompilerParams(
            collective_id=0, has_side_effects=True, vmem_limit_bytes=62 * 1024 * 1024
        ),
        cost_estimate=pl.CostEstimate(
            flops=3_000_000_000, bytes_accessed=12_000_000, transcendentals=1_200_000
        ),
    )(
        queries[0], keys[0], values[0], gates[0], cotangent[0], w_out, segment,
    )
    results = pl.pallas_call(
        hand_over,
        out_shape=tuple(jax.ShapeDtypeStruct(r.shape, r.dtype) for r in results),
        in_specs=[anywhere] * 6,
        out_specs=(anywhere,) * 6,
        scratch_shapes=[dma((6,))],
        compiler_params=pltpu.CompilerParams(vmem_limit_bytes=62 * 1024 * 1024),
        cost_estimate=pl.CostEstimate(flops=0, bytes_accessed=3_000_000, transcendentals=0),
    )(*results)
    output, dq, dk, dv, dgate, weight_grad = results
    if not fused:
        weight_grad = lax.psum_scatter(weight_grad, ("dp", "seq"), scatter_dimension=0, tiled=True)
    return output[None], dq[None], dk[None], dv[None], dgate[None], weight_grad


def solution(mesh):
    tokens = P("dp", "seq", None)
    return jax.shard_map(
        shards,
        mesh=mesh,
        in_specs=(tokens,) * 5 + (P("dp", None), P()),
        out_specs=(tokens,) * 5 + (P(("dp", "seq"), None),),
        check_vma=False,
    )
```
